32 devices in a mesh: groups: 2 (over y), blk: 4 (over z), occ: 2 (over x), sub: 2 (over core).
Axes of the slice: x: 2, y: 2, z: 4, core: 2. Of those that a mesh axis runs over, the one named last changes fastest.
Arguments:
- amplitudes: bfloat16 [512, 64], P(('groups', 'occ'), 'blk'), parts along dimension 0, may hold values from -6 to 6
- integrals: bfloat16 [401408, 64], P(('groups', 'blk', 'sub')), parts along dimension 0, may hold values from -0.75 to 0.75
Outputs:
- residual: float32 [512, 200704], P(('groups', 'occ'), ('blk', 'sub')), parts along dimension 0
The draws below stay inside these ranges and needn't reach their ends.
There are 2 independent parts, one for each index of `groups`. The reference program is written for one: setup_inputs(seed, part) draws one part's arguments, and reference() takes and returns one part's arrays. A program takes and returns all parts, laid end to end along the dimension named above; each array names one. Nothing has to cross between parts.
All inputs are finite; a program needn't handle non-finite values.
Results may differ from the reference program's by a relative error of at most 0.0003.
Values may be sent and summed in bfloat16 or wider, within the bound.
No kernel may reach another device: no remote copies, remote signals or barrier semaphores. Data moves between devices by JAX's collectives and lax.ppermute only.
A program may use at most 128 MiB of HBM per device.

```python
import jax
import jax.numpy as jnp
from jax import lax

NOCC = 16
NVIR = 448
KW = 64


def block_scale(rng, dims, cuts, smallest, largest):
    factor_of = 1.0
    for axis_at, shards_of in cuts:
        heights = jax.random.uniform(jax.random.fold_in(jax.random.fold_in(rng, 6), axis_at), (shards_of,), jnp.float32, smallest / len(cuts), largest / len(cuts))
        factor_of = factor_of * jnp.repeat(jnp.exp(heights), dims[axis_at] // shards_of).reshape((-1,) + (1,) * (len(dims) - 1 - axis_at))
    return factor_of


def normal_values(key, extent, scale, reach, pieces=(), held_as=jnp.bfloat16):
    loudness = block_scale(key, extent, pieces, -0.22, 0.18) if pieces else 1.0
    drawn = jax.random.normal(key, extent, jnp.float32) * scale * loudness
    return jnp.minimum(jnp.maximum(drawn, -reach), reach).astype(held_as)


def setup_inputs(seed: int = 0, part: int = 0) -> dict:
    keys = jax.random.split(jax.random.key(seed), 3)
    own_keys = jax.random.split(jax.random.fold_in(keys[2], part), 3)
    return {
        "amplitudes": normal_values(own_keys[0], (NOCC * NOCC, KW), 1.0, 6.0, ((0, 2), (1, 4))),
        "integrals": normal_values(own_keys[1], (NVIR * NVIR, KW), KW ** -0.5, 0.75, ((0, 8),)),
    }


def reference(amplitudes, integrals):
    ladder = lax.dot_general(amplitudes, integrals, (((1,), (1,)), ((), ())), preferred_element_type=jnp.float32)
    blocks = ladder.reshape(NOCC, NOCC, NVIR, NVIR)
    summed = blocks + jnp.transpose(blocks, (1, 0, 3, 2))
    return summed.reshape(NOCC * NOCC, NVIR * NVIR)
```

```python
import functools

import jax
import jax.numpy as jnp
from jax import lax
from jax.experimental import pallas as pl
from jax.experimental.pallas import tpu as pltpu
from jax.sharding import PartitionSpec as P

NOCC = 16
NVIR = 448
LANES = 128
VMEM = 56 * 2**20
NT = (((1,), (1,)), ((), ()))
NN = (((1,), (0,)), ((), ()))


def position():
    return lax.axis_index("blk") * 2 + lax.axis_index("sub"), lax.axis_index("occ")


def pack_kernel(plan, vt, *rest):
    outs, rows = rest[:-1], rest[-1]
    kw = vt.shape[0]
    vl = rows.shape[0]
    half = vl // 2
    tiles = 2 * NVIR // LANES
    me, plane = position()

    def turn(pair, carry):
        base = pl.multiple_of(pair * (2 * NVIR), LANES)
        for t in range(tiles):
            block = vt[:, pl.ds(pl.multiple_of(base + t * LANES, LANES), LANES)]
            turned = jnp.concatenate([block, block], axis=0).T.astype(jnp.float32)
            start = t * LANES
            if start + LANES <= NVIR:
                rows[2 * pair, start : start + LANES, :] = turned
            elif start >= NVIR:
                rows[2 * pair + 1, start - NVIR : start - NVIR + LANES, :] = turned
            else:
                cut = NVIR - start
                rows[2 * pair, start:NVIR, :] = turned[:cut]
                rows[2 * pair + 1, 0 : LANES - cut, :] = turned[cut:]
        return carry

    lax.fori_loop(0, vl // 2, turn, 0)
    low = lax.broadcasted_iota(jnp.int32, (vl, LANES), 1) < kw
    for out, (far, first, count, shared) in zip(outs, plan):
        base = jnp.bitwise_xor(me, far) * vl

        def gather(n, carry, out=out, base=base, first=first, shared=shared):
            if shared:
                m, at = 2 * (first + n) + plane, (n,)
            else:
                m, at = n, (n % 2, n // 2)
            for h in range(2):
                a = base + 2 * m + h
                both = jnp.where(low, rows[:, a, :], rows[:, a + half, :])
                out[(*at, slice(h * vl, (h + 1) * vl), slice(None))] = both.astype(jnp.bfloat16)
            return carry

        lax.fori_loop(0, count, gather, 0)


def pack(vt, plan, vl):
    shapes = []
    for _, _, count, shared in plan:
        lead = (count,) if shared else (2, count // 2)
        shapes.append(jax.ShapeDtypeStruct((*lead, 2 * vl, LANES), jnp.bfloat16))
    whole = pl.BlockSpec(memory_space=pltpu.VMEM)
    return pl.pallas_call(
        functools.partial(pack_kernel, plan),
        in_specs=[whole],
        out_specs=[whole] * len(plan),
        out_shape=shapes,
        scratch_shapes=[pltpu.VMEM((vl, NVIR, LANES), jnp.float32)],
        compiler_params=pltpu.CompilerParams(vmem_limit_bytes=VMEM),
        cost_estimate=pl.CostEstimate(flops=0, bytes_accessed=16 * 2**20, transcendentals=0),
    )(vt)


def combine_kernel(sources, first, count, own, n_prev, gathered, vt, *rest):
    arrivals = rest[: len(sources)]
    out = rest[len(sources) + n_prev]
    slot, lhs, direct, second, sems = rest[len(sources) + n_prev + 1 :]
    kw = vt.shape[0]
    pairs = out.shape[0]
    vl = slot.shape[3] // 2
    me, plane = position()
    i, xx, h = pl.program_id(0), pl.program_id(1), pl.program_id(2)

    @pl.when((i == 0) & (xx == 0) & (h == 0))
    def _():
        copies = []
        for n, (ref, (far, kind, start)) in enumerate(zip(arrivals, sources)):
            q = jnp.bitwise_xor(me, far)
            if kind == "both":
                copy = pltpu.make_async_copy(ref.at[:, pl.ds(start, count)], slot.at[q], sems.at[n])
            else:
                side = plane if kind == "own" else 1 - plane
                copy = pltpu.make_async_copy(ref.at[pl.ds(start, count)], slot.at[q, side], sems.at[n])
            copy.start()
            copies.append(copy)
        row = lax.broadcasted_iota(jnp.int32, (pairs, LANES), 0)
        col = lax.broadcasted_iota(jnp.int32, (pairs, LANES), 1)
        occ_i, occ_j = row // NOCC, row % NOCC
        per = pairs // NOCC
        zeros = jnp.zeros((kw, pairs), jnp.bfloat16)
        left = jnp.zeros((pairs, LANES), jnp.float32)
        right = jnp.zeros((pairs, LANES), jnp.float32)
        mine = jnp.zeros((pairs, kw), jnp.float32)
        for part in range(2):
            block = gathered[part * kw : (part + 1) * kw, :]
            swap = (occ_j // per == part) & (col == (occ_j % per) * NOCC + plane * per + occ_i)
            pick = jnp.where(swap, 1.0, 0.0).astype(jnp.bfloat16)
            left += lax.dot_general(pick, jnp.concatenate([block, zeros], axis=0), NT, preferred_element_type=jnp.float32)
            right += lax.dot_general(pick, jnp.concatenate([zeros, block], axis=0), NT, preferred_element_type=jnp.float32)
            keep = jnp.where((row == col) & (plane == part), 1.0, 0.0).astype(jnp.bfloat16)
            mine += lax.dot_general(keep, block, NT, preferred_element_type=jnp.float32)
        lhs[:pairs, :] = left.astype(jnp.bfloat16)
        lhs[pairs:, :] = right.astype(jnp.bfloat16)
        direct[...] = mine.astype(jnp.bfloat16)
        for copy in copies:
            copy.wait()

    ladder = lax.dot_general(direct[...], vt[...], NN, preferred_element_type=jnp.float32)

    @pl.when(h == 0)
    def _():
        blocks = [slot[q, xx, i].astype(jnp.float32) for q in range(slot.shape[0])]
        rows = [b[:vl] for b in blocks] + [b[vl:] for b in blocks]
        rhs = jnp.concatenate(rows, axis=0).astype(jnp.bfloat16)
        both = lax.dot_general(lhs[...], rhs, NT, preferred_element_type=jnp.float32)
        out[...] = ladder + both[:pairs]
        second[...] = both[pairs:]

    @pl.when(h == 1)
    def _():
        out[...] = ladder + second[...]


def combine(gathered, vt, arrivals, sources, first, count, previous, vl, pairs):
    n_dev = NVIR // vl
    steps = vl // 4
    width = 2 * NVIR
    any_space = pl.BlockSpec(memory_space=pl.ANY)

    def block(i, xx, h):
        return 0, 2 * (first + i) + xx + steps * h

    prev = [] if previous is None else [previous]
    return pl.pallas_call(
        functools.partial(combine_kernel, sources, first, count, None, len(prev)),
        grid=(count, 2, 2),
        in_specs=[
            pl.BlockSpec(gathered.shape, lambda i, xx, h: (0, 0)),
            pl.BlockSpec((vt.shape[0], width), block),
        ]
        + [any_space] * (len(arrivals) + len(prev)),
        out_specs=pl.BlockSpec((pairs, width), block),
        out_shape=jax.ShapeDtypeStruct((pairs, vl * NVIR), jnp.float32),
        scratch_shapes=[
            pltpu.VMEM((n_dev, 2, count, 2 * vl, LANES), jnp.bfloat16),
            pltpu.VMEM((2 * pairs, LANES), jnp.bfloat16),
            pltpu.VMEM((pairs, vt.shape[0]), jnp.bfloat16),
            pltpu.VMEM((pairs, width), jnp.float32),
            pltpu.SemaphoreType.DMA((len(sources),)),
        ],
        input_output_aliases={2 + len(arrivals): 0} if prev else {},
        compiler_params=pltpu.CompilerParams(vmem_limit_bytes=VMEM),
        cost_estimate=pl.CostEstimate(
            flops=8 * count * pairs * 3 * vt.shape[0] * width, bytes_accessed=count * 4 * pairs * width * 5, transcendentals=0
        ),
    )(gathered, vt, *arrivals, *prev)


def shards_fast(amplitudes, integrals):
    pairs = amplitudes.shape[0]
    vl = integrals.shape[0] // NVIR
    half = vl // 8
    late = 2
    early = half - late
    n_dev = NVIR // vl
    vt = integrals.T
    gathered = lax.all_gather(amplitudes.T, ("occ", "blk"), axis=0, tiled=True)

    def far_swap(x, far):
        return lax.ppermute(x, ("blk", "sub"), [(i, i ^ far) for i in range(n_dev)])

    def plane_swap(x):
        return lax.ppermute(x, "occ", [(0, 1), (1, 0)])

    center = pack(vt, [(4, 0, half, True), (5, 0, half, True), (6, 0, half, True), (7, 0, early, True), (7, early, late, True)], vl)
    near = pack(vt, [(f, 0, 2 * half, False) for f in range(4)], vl)
    got = [far_swap(x, f) for x, f in zip(center, (4, 5, 6, 7, 7))]
    forwarded = [plane_swap(x) for x in got]
    nears = [near[0]] + [far_swap(near[f], f) for f in (1, 2, 3)]

    def piece(start, count, last):
        arrivals, sources = [], []
        for f in range(4):
            arrivals.append(nears[f])
            sources.append((f, "both", start))
        for n, f in enumerate((4, 5, 6)):
            arrivals += [got[n], forwarded[n]]
            sources += [(f, "own", start), (f, "other", start)]
        arrivals += [got[last], forwarded[last]]
        sources += [(7, "own", 0), (7, "other", 0)]
        return arrivals, sources

    arrivals, sources = piece(0, early, 3)
    out = combine(gathered, vt, arrivals, sources, 0, early, None, vl, pairs)
    arrivals, sources = piece(early, late, 4)
    return combine(gathered, vt, arrivals, sources, early, late, out, vl, pairs)


def shards_any(amplitudes, integrals):
    pairs, columns = amplitudes.shape[0], integrals.shape[1]
    vl = integrals.shape[0] // NVIR
    per = pairs // NOCC
    swapped = lax.all_to_all(
        integrals.reshape(vl, NVIR, columns), ("blk", "sub"), split_axis=1, concat_axis=0, tiled=True
    )
    swapped = jnp.transpose(swapped, (1, 0, 2)).reshape(vl * NVIR, columns)
    whole = lax.all_gather(amplitudes, "blk", axis=1, tiled=True)
    every = lax.all_gather(whole, "occ", axis=0, tiled=True).reshape(NOCC, NOCC, columns)
    mine = lax.dynamic_slice_in_dim(every, lax.axis_index("occ") * per, per, axis=1)
    mine = jnp.transpose(mine, (1, 0, 2)).reshape(pairs, columns)
    return lax.dot_general(whole, integrals, NT, preferred_element_type=jnp.float32) + lax.dot_general(
        mine, swapped, NT, preferred_element_type=jnp.float32
    )


def shards(amplitudes, integrals):
    vl = integrals.shape[0] // NVIR
    fits = NVIR == 8 * vl and integrals.shape[1] * 2 == LANES and amplitudes.shape[0] == LANES
    fits = fits and lax.axis_size("blk") == 4 and lax.axis_size("sub") == 2 and lax.axis_size("occ") == 2
    return (shards_fast if fits else shards_any)(amplitudes, integrals)


def solution(mesh):
    placed = (P(("groups", "occ"), "blk"), P(("groups", "blk", "sub"), None))
    return jax.shard_map(
        shards,
        mesh=mesh,
        in_specs=placed,
        out_specs=P(("groups", "occ"), ("blk", "sub")),
        check_vma=False,
    )
```

```python
import functools

import jax
import jax.numpy as jnp
from jax import lax
from jax.experimental import pallas as pl
from jax.experimental.pallas import tpu as pltpu
from jax.sharding import PartitionSpec as P

NOCC = 16
NVIR = 448
LANES = 128
NT = (((1,), (1,)), ((), ()))
NN = (((1,), (0,)), ((), ()))


def position():
    return lax.axis_index("blk"), lax.axis_index("sub"), lax.axis_index("occ")


def far_of(cross, plane):
    return 2 * (2 + jnp.bitwise_xor(plane, cross)) + cross


def pack_kernel(plan, has_rider, vt, *rest):
    rider = rest[0] if has_rider else None
    outs = rest[has_rider : has_rider + len(plan)]
    local, rows, staged, in_sems, out_sems, rider_sem = rest[has_rider + len(plan) :]
    kw = vt.shape[0]
    vl = rows.shape[0]
    half = vl // 2
    tiles = 2 * NVIR // LANES
    chunks = in_sems.shape[0]
    per = vl // 2 // chunks
    z, core, plane = position()
    me = 2 * z + core

    def load(c):
        span = pl.ds(c * per * 2 * NVIR, per * 2 * NVIR)
        return pltpu.make_async_copy(vt.at[:, span], local.at[:, span], in_sems.at[c])

    for c in range(chunks):
        load(c).start()

    def turn(pair, carry):
        base = pl.multiple_of(pair * (2 * NVIR), LANES)
        for t in range(tiles):
            block = local[:, pl.ds(pl.multiple_of(base + t * LANES, LANES), LANES)]
            turned = jnp.concatenate([block, block], axis=0).T.astype(jnp.float32)
            start = t * LANES
            if start + LANES <= NVIR:
                rows[2 * pair, start : start + LANES, :] = turned
            elif start >= NVIR:
                rows[2 * pair + 1, start - NVIR : start - NVIR + LANES, :] = turned
            else:
                cut = NVIR - start
                rows[2 * pair, start:NVIR, :] = turned[:cut]
                rows[2 * pair + 1, 0 : LANES - cut, :] = turned[cut:]
        return carry

    for c in range(chunks):
        load(c).wait()
        lax.fori_loop(c * per, (c + 1) * per, turn, 0, unroll=True)

    low = lax.broadcasted_iota(jnp.int32, (vl, LANES), 1) < kw
    copies = []
    at = 0
    for n, (out, (kind, first, count, rides)) in enumerate(zip(outs, plan)):
        far = {"own": 0, "core": 1, "near": 2 + plane, "same": far_of(0, plane), "cross": far_of(1, plane)}[kind]
        base = jnp.bitwise_xor(me, far) * vl

        def gather(i, carry, base=base, first=first, at=at):
            both = []
            for h in range(2):
                a = base + 2 * (first + i) + h
                both.append(jnp.where(low, rows[:, a, :], rows[:, a + half, :]))
            spot = pl.multiple_of(at + i * 2 * vl, 16)
            staged[pl.ds(spot, 2 * vl), :] = jnp.concatenate(both, axis=0).astype(jnp.bfloat16)
            return carry

        lax.fori_loop(0, count, gather, 0)
        size = count * 2 * vl
        copy = pltpu.make_async_copy(staged.at[pl.ds(at, size)], out.at[pl.ds(0, size)], out_sems.at[n])
        copy.start()
        copies.append(copy)
        if rides:
            copy = pltpu.make_async_copy(rider, out.at[pl.ds(size, rider.shape[0])], rider_sem.at[n])
            copy.start()
            copies.append(copy)
        at += size
    for copy in copies:
        copy.wait()


def pack(vt, plan, vl, rider):
    sizes = [count * 2 * vl for _, _, count, _ in plan]
    extra = rider.shape[0]
    has_rider = any(rides for _, _, _, rides in plan)
    anywhere = pl.BlockSpec(memory_space=pl.ANY)
    chunks = 4
    return pl.pallas_call(
        functools.partial(pack_kernel, plan, has_rider),
        in_specs=[anywhere] * (1 + has_rider),
        out_specs=[anywhere] * len(plan),
        out_shape=[
            jax.ShapeDtypeStruct((size + extra * rides, LANES), jnp.bfloat16)
            for size, (_, _, _, rides) in zip(sizes, plan)
        ],
        scratch_shapes=[
            pltpu.VMEM(vt.shape, vt.dtype),
            pltpu.VMEM((vl, NVIR, LANES), jnp.float32),
            pltpu.VMEM((sum(sizes), LANES), jnp.bfloat16),
            pltpu.SemaphoreType.DMA((chunks,)),
            pltpu.SemaphoreType.DMA((len(plan),)),
            pltpu.SemaphoreType.DMA((len(plan),)),
        ],
        compiler_params=pltpu.CompilerParams(vmem_limit_bytes=24 * 2**20),
        cost_estimate=pl.CostEstimate(flops=0, bytes_accessed=16 * 2**20, transcendentals=0),
    )(vt, *([rider] if has_rider else []))


def amplitude_kernel(sides, own, others, tall, sems, z, plane):
    copies = [
        pltpu.make_async_copy(own, tall.at[plane, z], sems.at[0]),
        pltpu.make_async_copy(others[0], tall.at[1 - plane, z], sems.at[1]),
    ]
    for n, (ref, (kind, mine)) in enumerate(zip(others[1:], sides)):
        side = plane if mine else 1 - plane
        far = {"near": 1, "same": far_of(0, side) // 2, "cross": far_of(1, side) // 2}[kind]
        spot = tall.at[side, jnp.bitwise_xor(z, far)]
        size = spot.shape[0]
        copies.append(pltpu.make_async_copy(ref.at[pl.ds(ref.shape[0] - size, size)], spot, sems.at[2 + n]))
    return copies


def combine_kernel(sources, first, count, opening, vt, *rest):
    arrivals, rest = rest[: len(sources)], rest[len(sources) :]
    if opening:
        own, across, out, lhs, direct, slot, local, made, in_sems, vt_sems, out_sems, tall, tall_sems = rest
    else:
        lhs, direct, _, out, slot, local, made, in_sems, vt_sems, out_sems = rest
    kw = vt.shape[0]
    pairs = out.shape[0]
    vl = NVIR // slot.shape[0]
    steps = vl // 4
    width = 2 * NVIR
    z, core, plane = position()
    me = 2 * z + core

    copies = []
    for h in range(2):
        span = pl.ds((first + steps * h) * width, count * width)
        copies.append(pltpu.make_async_copy(vt.at[:, span], local.at[h], vt_sems.at[h]))
    for n, (ref, (kind, mine, start)) in enumerate(zip(arrivals, sources)):
        side = plane if mine else 1 - plane
        far = {"own": 0, "core": 1, "near": 2 + side, "same": far_of(0, side), "cross": far_of(1, side)}[kind]
        span = pl.ds(start * 2 * vl, count * 2 * vl)
        copies.append(pltpu.make_async_copy(ref.at[span], slot.at[jnp.bitwise_xor(me, far)], in_sems.at[n]))
    if opening:
        riders = [(ref, (kind, mine)) for ref, (kind, mine, _) in zip(arrivals, sources) if kind in ("near", "same", "cross")]
        gathers = amplitude_kernel([s for _, s in riders], own, [across] + [r for r, _ in riders], tall, tall_sems, z, plane)
        for copy in gathers + copies:
            copy.start()
        for copy in gathers:
            copy.wait()
        row = lax.broadcasted_iota(jnp.int32, (pairs, LANES), 0)
        col = lax.broadcasted_iota(jnp.int32, (pairs, LANES), 1)
        occ_i, occ_j = row // NOCC, row % NOCC
        per = pairs // NOCC
        zeros = jnp.zeros((kw, pairs), jnp.bfloat16)
        left = jnp.zeros((pairs, LANES), jnp.float32)
        right = jnp.zeros((pairs, LANES), jnp.float32)
        same = jnp.zeros((pairs, kw), jnp.float32)
        for part in range(2):
            block = tall[part].reshape(kw, pairs)
            swap = (occ_j // per == part) & (col == (occ_j % per) * NOCC + plane * per + occ_i)
            pick = jnp.where(swap, 1.0, 0.0).astype(jnp.bfloat16)
            left += lax.dot_general(pick, jnp.concatenate([block, zeros], axis=0), NT, preferred_element_type=jnp.float32)
            right += lax.dot_general(pick, jnp.concatenate([zeros, block], axis=0), NT, preferred_element_type=jnp.float32)
            keep = jnp.where((row == col) & (plane == part), 1.0, 0.0).astype(jnp.bfloat16)
            same += lax.dot_general(keep, block, NT, preferred_element_type=jnp.float32)
        lhs[:pairs, :] = left.astype(jnp.bfloat16)
        lhs[pairs:, :] = right.astype(jnp.bfloat16)
        direct[...] = same.astype(jnp.bfloat16)
    else:
        for copy in copies:
            copy.start()
    for copy in copies:
        copy.wait()

    def put(h, m):
        spot = pl.ds((first + m + steps * h) * width, width)
        return pltpu.make_async_copy(made.at[h, m], out.at[:, spot], out_sems.at[h, m])

    def step(m, carry):
        span = pl.ds(pl.multiple_of(m * 2 * vl, 16), 2 * vl)
        blocks = [slot[q, span, :].astype(jnp.float32) for q in range(slot.shape[0])]
        rhs = jnp.concatenate([b[:vl] for b in blocks] + [b[vl:] for b in blocks], axis=0).astype(jnp.bfloat16)
        both = lax.dot_general(lhs[...], rhs, NT, preferred_element_type=jnp.float32)
        for h in range(2):
            near = local[h, :, pl.ds(pl.multiple_of(m * width, LANES), width)]
            ladder = lax.dot_general(direct[...], near, NN, preferred_element_type=jnp.float32)
            made[h, m] = ladder + both[h * pairs : (h + 1) * pairs]
            put(h, m).start()
        return carry

    lax.fori_loop(0, count, step, 0)

    def finish(m, carry):
        for h in range(2):
            put(h, m).wait()
        return carry

    lax.fori_loop(0, count, finish, 0)


def combine(vt, arrivals, sources, first, count, vl, pairs, opening=None, later=None):
    kw, width, n_dev = vt.shape[0], 2 * NVIR, NVIR // vl
    anywhere = pl.BlockSpec(memory_space=pl.ANY)
    vmem = pl.BlockSpec(memory_space=pltpu.VMEM)
    out_shape = jax.ShapeDtypeStruct((pairs, vl * NVIR), jnp.float32)
    scratch = [
        pltpu.VMEM((n_dev, count * 2 * vl, LANES), jnp.bfloat16),
        pltpu.VMEM((2, kw, count * width), jnp.bfloat16),
        pltpu.VMEM((2, count, pairs, width), jnp.float32),
        pltpu.SemaphoreType.DMA((len(sources),)),
        pltpu.SemaphoreType.DMA((2,)),
        pltpu.SemaphoreType.DMA((2, count)),
    ]
    if opening is not None:
        extra = list(opening)
        specs = [anywhere] * 2
        outs = [out_shape, jax.ShapeDtypeStruct((2 * pairs, LANES), jnp.bfloat16), jax.ShapeDtypeStruct((pairs, kw), jnp.bfloat16)]
        out_specs = [anywhere, vmem, vmem]
        planes = 2
        scratch += [
            pltpu.VMEM((planes, kw // opening[0].shape[0], *opening[0].shape), jnp.bfloat16),
            pltpu.SemaphoreType.DMA((2 + len(sources),)),
        ]
        aliases = {}
    else:
        extra = list(later)
        specs = [vmem, vmem, anywhere]
        outs, out_specs = out_shape, anywhere
        aliases = {1 + len(arrivals) + 2: 0}
    return pl.pallas_call(
        functools.partial(combine_kernel, sources, first, count, opening is not None),
        in_specs=[anywhere] * (1 + len(arrivals)) + specs,
        out_specs=out_specs,
        out_shape=outs,
        scratch_shapes=scratch,
        input_output_aliases=aliases,
        compiler_params=pltpu.CompilerParams(vmem_limit_bytes=24 * 2**20),
        cost_estimate=pl.CostEstimate(
            flops=4 * count * pairs * 3 * kw * width, bytes_accessed=count * 2 * pairs * width * 6, transcendentals=0
        ),
    )(vt, *arrivals, *extra)


SIZES = (9, 5)


def shards_fast(amplitudes, integrals):
    pairs = amplitudes.shape[0]
    vl = integrals.shape[0] // NVIR
    steps = vl // 4
    vt = integrals.T
    own = amplitudes.T
    everyone = [(z, x, s) for z in range(4) for x in range(2) for s in range(2)]

    def number(z, x, s):
        return (z * 2 + x) * 2 + s

    def send(x, kind):
        def to(z, plane, s):
            if kind == "core":
                return number(z, plane, 1 - s)
            if kind == "plane":
                return number(z, 1 - plane, s)
            if kind == "near":
                return number(z ^ 1, plane, s ^ plane)
            cross = kind == "cross"
            return number(z ^ (2 + (plane ^ cross)), plane, s ^ cross)

        return lax.ppermute(x, ("blk", "occ", "sub"), [(number(*d), to(*d)) for d in everyone])

    across = send(own, "plane")
    spans, start = [], 0
    for size in SIZES:
        spans.append((start, size))
        start += size
    kinds = ("same", "cross")
    head = pack(vt, [(kind, *spans[0], True) for kind in kinds], vl, own)
    plan = [("near", 0, steps, True), ("core", 0, steps, False)]
    plan += [(kind, *span, False) for span in spans[1:] for kind in kinds]
    plan += [("own", 0, steps, False)]
    tail = pack(vt, plan, vl, own)
    near, core, mine = send(tail[0], "near"), send(tail[1], "core"), tail[-1]
    near_across = send(near, "plane")
    out = None
    for n, (first, count) in enumerate(spans):
        messages = head if n == 0 else tail[2 * n : 2 * n + 2]
        got = [send(x, kind) for x, kind in zip(messages, kinds)]
        passed = [send(x, "plane") for x in got]
        arrivals = [mine, core, near, near_across] + got + passed
        sources = [("own", True, first), ("core", True, first), ("near", True, first), ("near", False, first)]
        sources += [(kind, True, 0) for kind in kinds] + [(kind, False, 0) for kind in kinds]
        if n == 0:
            out, lhs, direct = combine(vt, arrivals, sources, first, count, vl, pairs, opening=(own, across))
        else:
            out = combine(vt, arrivals, sources, first, count, vl, pairs, later=(lhs, direct, out))
    return out


def shards_any(amplitudes, integrals):
    pairs, columns = amplitudes.shape[0], integrals.shape[1]
    vl = integrals.shape[0] // NVIR
    per = pairs // NOCC
    swapped = lax.all_to_all(
        integrals.reshape(vl, NVIR, columns), ("blk", "sub"), split_axis=1, concat_axis=0, tiled=True
    )
    swapped = jnp.transpose(swapped, (1, 0, 2)).reshape(vl * NVIR, columns)
    whole = lax.all_gather(amplitudes, "blk", axis=1, tiled=True)
    every = lax.all_gather(whole, "occ", axis=0, tiled=True).reshape(NOCC, NOCC, columns)
    mine = lax.dynamic_slice_in_dim(every, lax.axis_index("occ") * per, per, axis=1)
    mine = jnp.transpose(mine, (1, 0, 2)).reshape(pairs, columns)
    return lax.dot_general(whole, integrals, NT, preferred_element_type=jnp.float32) + lax.dot_general(
        mine, swapped, NT, preferred_element_type=jnp.float32
    )


def shards(amplitudes, integrals):
    vl = integrals.shape[0] // NVIR
    fits = NVIR == 8 * vl and integrals.shape[1] * 2 == LANES and amplitudes.shape[0] == LANES
    fits = fits and lax.axis_size("blk") == 4 and lax.axis_size("sub") == 2 and lax.axis_size("occ") == 2
    return (shards_fast if fits else shards_any)(amplitudes, integrals)


def solution(mesh):
    placed = (P(("groups", "occ"), "blk"), P(("groups", "blk", "sub"), None))
    return jax.shard_map(
        shards,
        mesh=mesh,
        in_specs=placed,
        out_specs=P(("groups", "occ"), ("blk", "sub")),
        check_vma=False,
    )
```

```python
import functools

import jax
import jax.numpy as jnp
from jax import lax
from jax.experimental import pallas as pl
from jax.experimental.pallas import tpu as pltpu
from jax.sharding import PartitionSpec as P

NOCC = 16
NVIR = 448
LANES = 128
NT = (((1,), (1,)), ((), ()))
NN = (((1,), (0,)), ((), ()))


def position():
    return lax.axis_index("blk"), lax.axis_index("sub"), lax.axis_index("occ")


def far_of(cross, plane):
    return 2 * (2 + jnp.bitwise_xor(plane, cross)) + cross


def pack_kernel(plan, opening, vt, *rest):
    if opening:
        amplitudes, outs, (local, rider) = rest[0], rest[1 : 1 + len(plan)], rest[1 + len(plan) : 3 + len(plan)]
        rows, in_sems, rider_sem = rest[3 + len(plan) :]
    else:
        outs, rows, local = rest[: len(plan)], rest[len(plan)], vt
    kw = vt.shape[0]
    vl = rows.shape[0]
    half = vl // 2
    tiles = 2 * NVIR // LANES
    chunks = in_sems.shape[0] if opening else 4
    per = vl // 2 // chunks
    z, core, plane = position()
    me = 2 * z + core

    def load(c):
        span = pl.ds(c * per * 2 * NVIR, per * 2 * NVIR)
        return pltpu.make_async_copy(vt.at[:, span], local.at[:, span], in_sems.at[c])

    if opening:
        for c in range(chunks):
            load(c).start()
        ride = pltpu.make_async_copy(amplitudes, rider, rider_sem)
        ride.start()

    def turn(pair, carry):
        base = pl.multiple_of(pair * (2 * NVIR), LANES)
        for t in range(tiles):
            block = local[:, pl.ds(pl.multiple_of(base + t * LANES, LANES), LANES)]
            turned = jnp.concatenate([block, block], axis=0).T.astype(jnp.float32)
            start = t * LANES
            if start + LANES <= NVIR:
                rows[2 * pair, start : start + LANES, :] = turned
            elif start >= NVIR:
                rows[2 * pair + 1, start - NVIR : start - NVIR + LANES, :] = turned
            else:
                cut = NVIR - start
                rows[2 * pair, start:NVIR, :] = turned[:cut]
                rows[2 * pair + 1, 0 : LANES - cut, :] = turned[cut:]
        return carry

    for c in range(chunks):
        if opening:
            load(c).wait()
        lax.fori_loop(c * per, (c + 1) * per, turn, 0, unroll=True)
    if opening:
        ride.wait()

    low = lax.broadcasted_iota(jnp.int32, (vl, LANES), 1) < kw
    for out, (kind, first, count, rides) in zip(outs, plan):
        far = {"own": 0, "core": 1, "near": 2 + plane, "same": far_of(0, plane), "cross": far_of(1, plane)}[kind]
        base = jnp.bitwise_xor(me, far) * vl

        def gather(i, carry, out=out, base=base, first=first):
            both = []
            for h in range(2):
                a = base + 2 * (first + i) + h
                both.append(jnp.where(low, rows[:, a, :], rows[:, a + half, :]))
            spot = pl.multiple_of(i * 2 * vl, 16)
            out[pl.ds(spot, 2 * vl), :] = jnp.concatenate(both, axis=0).astype(jnp.bfloat16)
            return carry

        lax.fori_loop(0, count, gather, 0)
        if rides:
            out[count * 2 * vl :, :] = rider[...]


def pack(vt, plan, vl, amplitudes=None):
    extra = 0 if amplitudes is None else amplitudes.shape[0]
    opening = amplitudes is not None
    vmem = pl.BlockSpec(memory_space=pltpu.VMEM)
    anywhere = pl.BlockSpec(memory_space=pl.ANY)
    chunks = 4
    shapes = [
        jax.ShapeDtypeStruct((count * 2 * vl + extra * rides, LANES), jnp.bfloat16) for _, _, count, rides in plan
    ]
    scratch = [pltpu.VMEM((vl, NVIR, LANES), jnp.float32)]
    if opening:
        shapes += [jax.ShapeDtypeStruct(x.shape, x.dtype) for x in (vt, amplitudes)]
        scratch += [pltpu.SemaphoreType.DMA((chunks,)), pltpu.SemaphoreType.DMA]
    return pl.pallas_call(
        functools.partial(pack_kernel, plan, opening),
        in_specs=[anywhere, anywhere] if opening else [vmem],
        out_specs=[vmem] * len(shapes),
        out_shape=shapes,
        scratch_shapes=scratch,
        compiler_params=pltpu.CompilerParams(vmem_limit_bytes=(HEAD_MB if opening else 20) * 2**20),
        cost_estimate=pl.CostEstimate(flops=0, bytes_accessed=PACK_COST * 2**20, transcendentals=0),
    )(vt, *([amplitudes] if opening else []))


def combine_kernel(sources, first, count, opening, vt, *rest):
    arrivals, rest = rest[: len(sources)], rest[len(sources) :]
    if opening:
        own, across, out, lhs, direct, turned, made, out_sems, tall = rest
    else:
        lhs, direct, _, out, turned, made, out_sems = rest
    kw = vt.shape[0]
    pairs = out.shape[0]
    n_dev = turned.shape[1] // 2
    vl = NVIR // n_dev
    steps = vl // 4
    width = 2 * NVIR
    z, core, plane = position()
    me = 2 * z + core

    def far(kind, side):
        return {"own": 0, "core": 1, "near": 2 + side, "same": far_of(0, side), "cross": far_of(1, side)}[kind]

    if opening:
        size = own.shape[0]
        tall[plane, z] = own[...]
        tall[1 - plane, z] = across[...]
        for ref, (kind, mine, start, at, _) in zip(arrivals, sources):
            if kind in ("near", "same", "cross") and start == 0 and at == 0:
                side = plane if mine else 1 - plane
                there = jnp.bitwise_xor(z, 1 if kind == "near" else far(kind, side) // 2)
                tall[side, there] = ref[ref.shape[0] - size :, :]
        row = lax.broadcasted_iota(jnp.int32, (pairs, LANES), 0)
        col = lax.broadcasted_iota(jnp.int32, (pairs, LANES), 1)
        occ_i, occ_j = row // NOCC, row % NOCC
        per = pairs // NOCC
        zeros = jnp.zeros((kw, pairs), jnp.bfloat16)
        left = jnp.zeros((pairs, LANES), jnp.float32)
        right = jnp.zeros((pairs, LANES), jnp.float32)
        same = jnp.zeros((pairs, kw), jnp.float32)
        for part in range(2):
            block = tall[part].reshape(kw, pairs)
            swap = (occ_j // per == part) & (col == (occ_j % per) * NOCC + plane * per + occ_i)
            pick = jnp.where(swap, 1.0, 0.0).astype(jnp.bfloat16)
            left += lax.dot_general(pick, jnp.concatenate([block, zeros], axis=0), NT, preferred_element_type=jnp.float32)
            right += lax.dot_general(pick, jnp.concatenate([zeros, block], axis=0), NT, preferred_element_type=jnp.float32)
            keep = jnp.where((row == col) & (plane == part), 1.0, 0.0).astype(jnp.bfloat16)
            same += lax.dot_general(keep, block, NT, preferred_element_type=jnp.float32)
        lhs[:pairs, :] = left.astype(jnp.bfloat16)
        lhs[pairs:, :] = right.astype(jnp.bfloat16)
        direct[...] = same.astype(jnp.bfloat16)

    def put(h, m):
        spot = pl.ds((first + m + steps * h) * width, width)
        return pltpu.make_async_copy(made.at[h, m], out.at[:, spot], out_sems.at[h, m])

    for m in range(count):
        buffer = turned.at[m % turned.shape[0]]
        for ref, (kind, mine, start, at, size) in zip(arrivals, sources):
            if at <= m < at + size:
                q = jnp.bitwise_xor(me, far(kind, plane if mine else 1 - plane))
                block = ref[(start + m - at) * 2 * vl : (start + m - at + 1) * 2 * vl, :].astype(jnp.float32)
                buffer[q] = block[:vl]
                buffer[q + n_dev] = block[vl:]
        rhs = buffer[...].reshape(2 * NVIR, LANES).astype(jnp.bfloat16)
        both = lax.dot_general(lhs[...], rhs, NT, preferred_element_type=jnp.float32)
        for h in range(2):
            begin = (first + m + steps * h) * width
            ladder = lax.dot_general(direct[...], vt[:, begin : begin + width], NN, preferred_element_type=jnp.float32)
            made[h, m] = ladder + both[h * pairs : (h + 1) * pairs]
            put(h, m).start()
    for m in range(count):
        for h in range(2):
            put(h, m).wait()


def combine(vt, arrivals, sources, first, count, vl, pairs, opening=None, later=None):
    kw, width, n_dev = vt.shape[0], 2 * NVIR, NVIR // vl
    anywhere = pl.BlockSpec(memory_space=pl.ANY)
    vmem = pl.BlockSpec(memory_space=pltpu.VMEM)
    out_shape = jax.ShapeDtypeStruct((pairs, vl * NVIR), jnp.float32)
    scratch = [
        pltpu.VMEM((2, 2 * n_dev, vl, LANES), jnp.float32),
        pltpu.VMEM((2, count, pairs, width), jnp.float32),
        pltpu.SemaphoreType.DMA((2, count)),
    ]
    if opening is not None:
        extra = list(opening)
        specs = [vmem] * 2
        outs = [out_shape, jax.ShapeDtypeStruct((2 * pairs, LANES), jnp.bfloat16), jax.ShapeDtypeStruct((pairs, kw), jnp.bfloat16)]
        out_specs = [anywhere, vmem, vmem]
        scratch += [pltpu.VMEM((2, kw // opening[0].shape[0], *opening[0].shape), jnp.bfloat16)]
        aliases = {}
    else:
        extra = list(later)
        specs = [vmem, vmem, anywhere]
        outs, out_specs = out_shape, anywhere
        aliases = {1 + len(arrivals) + 2: 0}
    return pl.pallas_call(
        functools.partial(combine_kernel, sources, first, count, opening is not None),
        in_specs=[vmem] * (1 + len(arrivals)) + specs,
        out_specs=out_specs,
        out_shape=outs,
        scratch_shapes=scratch,
        input_output_aliases=aliases,
        compiler_params=pltpu.CompilerParams(vmem_limit_bytes=20 * 2**20),
        cost_estimate=pl.CostEstimate(
            flops=4 * count * pairs * 3 * kw * width, bytes_accessed=count * 2 * pairs * width * 6, transcendentals=0
        ),
    )(vt, *arrivals, *extra)


HEAD_MB = 54
PACK_COST = 16
FLOWS = (('same', 0, 6, None), ('cross', 0, 9, None), ('near', 0, 14, None), ('same', 6, 5, 0), ('cross', 9, 5, 1), ('same', 11, 3, 3))
PIECES = ((0, 9), (9, 5))


def shards_fast(amplitudes, integrals):
    pairs = amplitudes.shape[0]
    vl = integrals.shape[0] // NVIR
    steps = vl // 4
    everyone = [(z, x, s) for z in range(4) for x in range(2) for s in range(2)]

    def number(z, x, s):
        return (z * 2 + x) * 2 + s

    def send(x, kind):
        def to(z, plane, s):
            if kind == "core":
                return number(z, plane, 1 - s)
            if kind == "plane":
                return number(z, 1 - plane, s)
            if kind == "near":
                return number(z ^ 1, plane, s ^ plane)
            cross = kind == "cross"
            return number(z ^ (2 + (plane ^ cross)), plane, s ^ cross)

        return lax.ppermute(x, ("blk", "occ", "sub"), [(number(*d), to(*d)) for d in everyone])

    def before(first, then):
        return lax.optimization_barrier((first, then))

    across = send(amplitudes.T, "plane")
    heads = [f for f, flow in enumerate(FLOWS) if flow[3] is None]
    tails = [f for f, flow in enumerate(FLOWS) if flow[3] is not None]
    plan = [(*FLOWS[f][:3], FLOWS[f][1] == 0) for f in heads]
    *packed, vt, own = pack(integrals.T, plan, vl, amplitudes.T)
    messages = dict(zip(heads, packed))
    across, messages[0] = before(across, messages[0])
    plan = [("core", 0, steps, False), ("own", 0, steps, False)] + [(*FLOWS[f][:3], False) for f in tails]
    core, mine, *packed = pack(vt, plan, vl)
    messages.update(zip(tails, packed))
    core = send(core, "core")
    got = []
    for f, (kind, _, _, after) in enumerate(FLOWS):
        if after is not None:
            got[after], messages[f] = before(got[after], messages[f])
        got.append(send(messages[f], kind))
    passed = [send(x, "plane") for x in got]
    out = None
    for n, (first, count) in enumerate(PIECES):
        arrivals = [mine, core]
        sources = [("own", True, first, 0, count), ("core", True, first, 0, count)]
        for flow, (kind, start, size, _) in enumerate(FLOWS):
            low, high = max(first, start), min(first + count, start + size)
            if low < high:
                arrivals += [got[flow], passed[flow]]
                span = (low - start, low - first, high - low)
                sources += [(kind, True, *span), (kind, False, *span)]
        if n == 0:
            out, lhs, direct = combine(vt, arrivals, sources, first, count, vl, pairs, opening=(own, across))
        else:
            out = combine(vt, arrivals, sources, first, count, vl, pairs, later=(lhs, direct, out))
    return out


def shards_any(amplitudes, integrals):
    pairs, columns = amplitudes.shape[0], integrals.shape[1]
    vl = integrals.shape[0] // NVIR
    per = pairs // NOCC
    swapped = lax.all_to_all(
        integrals.reshape(vl, NVIR, columns), ("blk", "sub"), split_axis=1, concat_axis=0, tiled=True
    )
    swapped = jnp.transpose(swapped, (1, 0, 2)).reshape(vl * NVIR, columns)
    whole = lax.all_gather(amplitudes, "blk", axis=1, tiled=True)
    every = lax.all_gather(whole, "occ", axis=0, tiled=True).reshape(NOCC, NOCC, columns)
    mine = lax.dynamic_slice_in_dim(every, lax.axis_index("occ") * per, per, axis=1)
    mine = jnp.transpose(mine, (1, 0, 2)).reshape(pairs, columns)
    return lax.dot_general(whole, integrals, NT, preferred_element_type=jnp.float32) + lax.dot_general(
        mine, swapped, NT, preferred_element_type=jnp.float32
    )


def shards(amplitudes, integrals):
    vl = integrals.shape[0] // NVIR
    fits = NVIR == 8 * vl and integrals.shape[1] * 2 == LANES and amplitudes.shape[0] == LANES
    fits = fits and lax.axis_size("blk") == 4 and lax.axis_size("sub") == 2 and lax.axis_size("occ") == 2
    return (shards_fast if fits else shards_any)(amplitudes, integrals)


def solution(mesh):
    placed = (P(("groups", "occ"), "blk"), P(("groups", "blk", "sub"), None))
    return jax.shard_map(
        shards,
        mesh=mesh,
        in_specs=placed,
        out_specs=P(("groups", "occ"), ("blk", "sub")),
        check_vma=False,
    )
```

```python
import functools

import jax
import jax.numpy as jnp
from jax import lax
from jax.experimental import pallas as pl
from jax.experimental.pallas import tpu as pltpu
from jax.sharding import PartitionSpec as P

NOCC = 16
NVIR = 448
LANES = 128
NT = (((1,), (1,)), ((), ()))
NN = (((1,), (0,)), ((), ()))


def position():
    return lax.axis_index("blk"), lax.axis_index("sub"), lax.axis_index("occ")


def far_of(cross, plane):
    return 2 * (2 + jnp.bitwise_xor(plane, cross)) + cross


def pack_kernel(plan, opening, vt, amplitudes, *rest):
    if not opening:
        across, *rest = rest
    outs, rest = rest[: len(plan)], rest[len(plan) :]
    if opening:
        local, rider, rows, in_sems, rider_sem = rest
        riders = [rider]
    else:
        (rows,), local, riders = rest, vt, [amplitudes, across]
    kw = vt.shape[0]
    vl = rows.shape[0]
    half = vl // 2
    tiles = 2 * NVIR // LANES
    chunks = in_sems.shape[0] if opening else 4
    per = vl // 2 // chunks
    z, core, plane = position()
    me = 2 * z + core

    def load(c):
        span = pl.ds(c * per * 2 * NVIR, per * 2 * NVIR)
        return pltpu.make_async_copy(vt.at[:, span], local.at[:, span], in_sems.at[c])

    if opening:
        for c in range(chunks):
            load(c).start()
        ride = pltpu.make_async_copy(amplitudes, rider, rider_sem)
        ride.start()

    def turn(pair, carry):
        base = pl.multiple_of(pair * (2 * NVIR), LANES)
        for t in range(tiles):
            block = local[:, pl.ds(pl.multiple_of(base + t * LANES, LANES), LANES)]
            turned = jnp.concatenate([block, block], axis=0).T.astype(jnp.float32)
            start = t * LANES
            if start + LANES <= NVIR:
                rows[2 * pair, start : start + LANES, :] = turned
            elif start >= NVIR:
                rows[2 * pair + 1, start - NVIR : start - NVIR + LANES, :] = turned
            else:
                cut = NVIR - start
                rows[2 * pair, start:NVIR, :] = turned[:cut]
                rows[2 * pair + 1, 0 : LANES - cut, :] = turned[cut:]
        return carry

    for c in range(chunks):
        if opening:
            load(c).wait()
        lax.fori_loop(c * per, (c + 1) * per, turn, 0, unroll=True)
    if opening:
        ride.wait()

    low = lax.broadcasted_iota(jnp.int32, (vl, LANES), 1) < kw
    for out, (kind, first, count, rides) in zip(outs, plan):
        far = {"own": 0, "core": 1, "near": 2 + plane, "near_same": 2, "near_cross": 3, "same": far_of(0, plane), "cross": far_of(1, plane)}[kind]
        base = jnp.bitwise_xor(me, far) * vl

        def gather(i, carry, out=out, base=base, first=first):
            both = []
            for h in range(2):
                a = base + 2 * (first + i) + h
                both.append(jnp.where(low, rows[:, a, :], rows[:, a + half, :]))
            spot = pl.multiple_of(i * 2 * vl, 16)
            out[pl.ds(spot, 2 * vl), :] = jnp.concatenate(both, axis=0).astype(jnp.bfloat16)
            return carry

        lax.fori_loop(0, count, gather, 0)
        for n in range(rides):
            size = riders[n].shape[0]
            begin = count * 2 * vl + n * size
            out[begin : begin + size, :] = riders[n][...]


def pack(vt, plan, vl, amplitudes, across=None):
    extra = amplitudes.shape[0]
    opening = across is None
    vmem = pl.BlockSpec(memory_space=pltpu.VMEM)
    anywhere = pl.BlockSpec(memory_space=pl.ANY)
    chunks = 4
    shapes = [
        jax.ShapeDtypeStruct((count * 2 * vl + extra * rides, LANES), jnp.bfloat16) for _, _, count, rides in plan
    ]
    scratch = [pltpu.VMEM((vl, NVIR, LANES), jnp.float32)]
    if opening:
        shapes += [jax.ShapeDtypeStruct(x.shape, x.dtype) for x in (vt, amplitudes)]
        scratch += [pltpu.SemaphoreType.DMA((chunks,)), pltpu.SemaphoreType.DMA]
    return pl.pallas_call(
        functools.partial(pack_kernel, plan, opening),
        in_specs=[anywhere] * 2 if opening else [vmem] * 3,
        out_specs=[vmem] * len(shapes),
        out_shape=shapes,
        scratch_shapes=scratch,
        compiler_params=pltpu.CompilerParams(vmem_limit_bytes=(HEAD_MB if opening else 20) * 2**20),
        cost_estimate=pl.CostEstimate(flops=0, bytes_accessed=PACK_COST * 2**10, transcendentals=0),
    )(vt, amplitudes, *([] if opening else [across]))


def combine_kernel(sources, first, count, opening, vt, *rest):
    arrivals, rest = rest[: len(sources)], rest[len(sources) :]
    if opening:
        own, across, out, lhs, direct, turned, made, out_sems, tall = rest
    else:
        lhs, direct, _, out, turned, made, out_sems = rest
    kw = vt.shape[0]
    pairs = out.shape[0]
    n_dev = turned.shape[1] // 2
    vl = NVIR // n_dev
    steps = vl // 4
    width = 2 * NVIR
    z, core, plane = position()
    me = 2 * z + core

    def far(kind, side):
        return {"own": 0, "core": 1, "near": 2 + side, "near_same": 2, "near_cross": 3, "same": far_of(0, side), "cross": far_of(1, side)}[kind]

    if opening:
        size = own.shape[0]
        tall[plane, z] = own[...]
        tall[1 - plane, z] = across[...]
        for ref, (kind, mine, start, at, _) in zip(arrivals, sources):
            if kind in ("near", "near_cross", "same", "cross") and start == 0 and at == 0:
                side = plane if mine else 1 - plane
                there = jnp.bitwise_xor(z, 1 if kind.startswith("near") else far(kind, side) // 2)
                if kind == "near_cross":
                    tall[1 - side, there] = ref[ref.shape[0] - size :, :]
                    tall[side, there] = ref[ref.shape[0] - 2 * size : ref.shape[0] - size, :]
                else:
                    tall[side, there] = ref[ref.shape[0] - size :, :]
        row = lax.broadcasted_iota(jnp.int32, (pairs, LANES), 0)
        col = lax.broadcasted_iota(jnp.int32, (pairs, LANES), 1)
        occ_i, occ_j = row // NOCC, row % NOCC
        per = pairs // NOCC
        zeros = jnp.zeros((kw, pairs), jnp.bfloat16)
        left = jnp.zeros((pairs, LANES), jnp.float32)
        right = jnp.zeros((pairs, LANES), jnp.float32)
        same = jnp.zeros((pairs, kw), jnp.float32)
        for part in range(2):
            block = tall[part].reshape(kw, pairs)
            swap = (occ_j // per == part) & (col == (occ_j % per) * NOCC + plane * per + occ_i)
            pick = jnp.where(swap, 1.0, 0.0).astype(jnp.bfloat16)
            left += lax.dot_general(pick, jnp.concatenate([block, zeros], axis=0), NT, preferred_element_type=jnp.float32)
            right += lax.dot_general(pick, jnp.concatenate([zeros, block], axis=0), NT, preferred_element_type=jnp.float32)
            keep = jnp.where((row == col) & (plane == part), 1.0, 0.0).astype(jnp.bfloat16)
            same += lax.dot_general(keep, block, NT, preferred_element_type=jnp.float32)
        lhs[:pairs, :] = left.astype(jnp.bfloat16)
        lhs[pairs:, :] = right.astype(jnp.bfloat16)
        direct[...] = same.astype(jnp.bfloat16)

    def put(h, m):
        spot = pl.ds((first + m + steps * h) * width, width)
        return pltpu.make_async_copy(made.at[h, m], out.at[:, spot], out_sems.at[h, m])

    for m in range(count):
        buffer = turned.at[m % turned.shape[0]]
        for ref, (kind, mine, start, at, size) in zip(arrivals, sources):
            if at <= m < at + size:
                q = jnp.bitwise_xor(me, far(kind, plane if mine else 1 - plane))
                block = ref[(start + m - at) * 2 * vl : (start + m - at + 1) * 2 * vl, :].astype(jnp.float32)
                buffer[q] = block[:vl]
                buffer[q + n_dev] = block[vl:]
        rhs = buffer[...].reshape(2 * NVIR, LANES).astype(jnp.bfloat16)
        both = lax.dot_general(lhs[...], rhs, NT, preferred_element_type=jnp.float32)
        for h in range(2):
            begin = (first + m + steps * h) * width
            ladder = lax.dot_general(direct[...], vt[:, begin : begin + width], NN, preferred_element_type=jnp.float32)
            made[h, m] = ladder + both[h * pairs : (h + 1) * pairs]
            put(h, m).start()
    for m in range(count):
        for h in range(2):
            put(h, m).wait()


def combine(vt, arrivals, sources, first, count, vl, pairs, opening=None, later=None):
    kw, width, n_dev = vt.shape[0], 2 * NVIR, NVIR // vl
    anywhere = pl.BlockSpec(memory_space=pl.ANY)
    vmem = pl.BlockSpec(memory_space=pltpu.VMEM)
    out_shape = jax.ShapeDtypeStruct((pairs, vl * NVIR), jnp.float32)
    scratch = [
        pltpu.VMEM((2, 2 * n_dev, vl, LANES), jnp.float32),
        pltpu.VMEM((2, count, pairs, width), jnp.float32),
        pltpu.SemaphoreType.DMA((2, count)),
    ]
    if opening is not None:
        extra = list(opening)
        specs = [vmem] * 2
        outs = [out_shape, jax.ShapeDtypeStruct((2 * pairs, LANES), jnp.bfloat16), jax.ShapeDtypeStruct((pairs, kw), jnp.bfloat16)]
        out_specs = [anywhere, vmem, vmem]
        scratch += [pltpu.VMEM((2, kw // opening[0].shape[0], *opening[0].shape), jnp.bfloat16)]
        aliases = {}
    else:
        extra = list(later)
        specs = [vmem, vmem, anywhere]
        outs, out_specs = out_shape, anywhere
        aliases = {1 + len(arrivals) + 2: 0}
    return pl.pallas_call(
        functools.partial(combine_kernel, sources, first, count, opening is not None),
        in_specs=[vmem] * (1 + len(arrivals)) + specs,
        out_specs=out_specs,
        out_shape=outs,
        scratch_shapes=scratch,
        input_output_aliases=aliases,
        compiler_params=pltpu.CompilerParams(vmem_limit_bytes=20 * 2**20),
        cost_estimate=pl.CostEstimate(flops=0, bytes_accessed=JOIN_COST * 2**10, transcendentals=0),
    )(vt, *arrivals, *extra)


HEAD_MB = 48
PACK_COST = 1
JOIN_COST = 1
FLOWS = (('same', 0, 6, 1), ('cross', 0, 9, 1), ('near', 0, 14, 1), ('same', 6, 5, 0), ('same', 11, 3, 0), ('cross', 9, 5, 0))
PIECES = ((0, 6), (6, 3), (9, 5))
AFTER = (('z3', ('z0',)), ('z5', ('z1',)), ('z4', ('x0',)), ('x0', ('across',)), ('x1', ('x0',)))


def shards_fast(amplitudes, integrals):
    pairs = amplitudes.shape[0]
    vl = integrals.shape[0] // NVIR
    steps = vl // 4
    everyone = [(z, x, s) for z in range(4) for x in range(2) for s in range(2)]

    def number(z, x, s):
        return (z * 2 + x) * 2 + s

    def send(x, kind):
        def to(z, plane, s):
            if kind == "core":
                return number(z, plane, 1 - s)
            if kind == "plane":
                return number(z, 1 - plane, s)
            if kind == "near":
                return number(z ^ 1, plane, s ^ plane)
            if kind in ("near_same", "near_cross"):
                return number(z ^ 1, plane, s ^ (kind == "near_cross"))
            cross = kind == "cross"
            return number(z ^ (2 + (plane ^ cross)), plane, s ^ cross)

        return lax.ppermute(x, ("blk", "occ", "sub"), [(number(*d), to(*d)) for d in everyone])

    values, after = {}, dict(AFTER)

    def hold(x, name):
        for first in after.get(name, ()):
            values[first], x = lax.optimization_barrier((result(first), x))
        return x

    def riders(f):
        kind, first = FLOWS[f][:2]
        return 0 if first or kind == "near_same" else 2 if kind == "near_cross" else 1

    def sources_of(first, count):
        names, sources = ["own", "core"], [("own", True, first, 0, count), ("core", True, first, 0, count)]
        for f, (kind, start, size, _) in enumerate(FLOWS):
            low, high = max(first, start), min(first + count, start + size)
            if low < high:
                span = (low - start, low - first, high - low)
                names.append(f"z{f}")
                sources.append((kind, True, *span))
                if kind in ("near", "same", "cross"):
                    names.append(f"x{f}")
                    sources.append((kind, False, *span))
        return names, sources

    def result(name):
        if name not in values:
            values[name] = make(name)
        return values[name]

    def make(name):
        index = int(name[1:]) if name[1:].isdigit() else None
        if name == "across":
            return send(hold(amplitudes.T, name), "plane")
        if name == "head":
            plan = [(*flow[:3], riders(f)) for f, flow in enumerate(FLOWS) if flow[3]]
            return pack(integrals.T, plan, vl, amplitudes.T)
        if name == "tail":
            plan = [("core", 0, steps, 0), ("own", 0, steps, 0)]
            plan += [(*flow[:3], riders(f)) for f, flow in enumerate(FLOWS) if not flow[3]]
            *_, vt, own = result("head")
            return pack(vt, plan, vl, hold(own, name), result("across"))
        if name == "tail_core":
            return result("tail")[0]
        if name == "own":
            return result("tail")[1]
        if name == "core":
            return send(hold(result("tail")[0], name), "core")
        if name[0] == "z":
            kind, _, _, head = FLOWS[index]
            place = sum(flow[3] == head for flow in FLOWS[:index])
            message = result("head")[place] if head else result("tail")[2 + place]
            return send(hold(message, name), kind)
        if name[0] == "x":
            return send(hold(result(f"z{index}"), name), "plane")
        if name[0] == "l":
            return result(f"k{index}")[1]
        first, count = PIECES[index]
        names, sources = sources_of(first, count)
        *_, vt, own = result("head")
        arrivals = [result(n) for n in names]
        if index == 0:
            return combine(vt, arrivals, sources, first, count, vl, pairs, opening=(own, result("across")))
        out = result(f"k{index - 1}")
        previous = out[0] if index == 1 else out
        return combine(vt, arrivals, sources, first, count, vl, pairs, later=(result("l0"), result("k0")[2], previous))

    return result(f"k{len(PIECES) - 1}")


def shards_any(amplitudes, integrals):
    pairs, columns = amplitudes.shape[0], integrals.shape[1]
    vl = integrals.shape[0] // NVIR
    per = pairs // NOCC
    swapped = lax.all_to_all(
        integrals.reshape(vl, NVIR, columns), ("blk", "sub"), split_axis=1, concat_axis=0, tiled=True
    )
    swapped = jnp.transpose(swapped, (1, 0, 2)).reshape(vl * NVIR, columns)
    whole = lax.all_gather(amplitudes, "blk", axis=1, tiled=True)
    every = lax.all_gather(whole, "occ", axis=0, tiled=True).reshape(NOCC, NOCC, columns)
    mine = lax.dynamic_slice_in_dim(every, lax.axis_index("occ") * per, per, axis=1)
    mine = jnp.transpose(mine, (1, 0, 2)).reshape(pairs, columns)
    return lax.dot_general(whole, integrals, NT, preferred_element_type=jnp.float32) + lax.dot_general(
        mine, swapped, NT, preferred_element_type=jnp.float32
    )


def shards(amplitudes, integrals):
    vl = integrals.shape[0] // NVIR
    fits = NVIR == 8 * vl and integrals.shape[1] * 2 == LANES and amplitudes.shape[0] == LANES
    fits = fits and lax.axis_size("blk") == 4 and lax.axis_size("sub") == 2 and lax.axis_size("occ") == 2
    return (shards_fast if fits else shards_any)(amplitudes, integrals)


def solution(mesh):
    placed = (P(("groups", "occ"), "blk"), P(("groups", "blk", "sub"), None))
    return jax.shard_map(
        shards,
        mesh=mesh,
        in_specs=placed,
        out_specs=P(("groups", "occ"), ("blk", "sub")),
        check_vma=False,
    )
```

```python
import functools

import jax
import jax.numpy as jnp
from jax import lax
from jax.experimental import pallas as pl
from jax.experimental.pallas import tpu as pltpu
from jax.sharding import PartitionSpec as P

NOCC = 16
NVIR = 448
LANES = 128
NT = (((1,), (1,)), ((), ()))
NN = (((1,), (0,)), ((), ()))

MESSAGES = (
    ("same", 0, 6, True),
    ("cross", 0, 10, True),
    ("near", 0, 14, True),
    ("same", 6, 5, False),
    ("same", 11, 3, False),
    ("cross", 10, 4, False),
)
PIECES = ((0, 6), (6, 4), (10, 4))
AFTER = {"z3": ("z0",), "z5": ("z1",), "z4": ("x0",), "x1": ("x0",), "tail": ("across",)}


def position():
    return lax.axis_index("blk"), lax.axis_index("sub"), lax.axis_index("occ")


def far_of(kind, plane):
    if kind == "own":
        return 0
    if kind == "core":
        return 1
    if kind == "near":
        return 2 + plane
    cross = int(kind == "cross")
    return 2 * (2 + jnp.bitwise_xor(plane, cross)) + cross


def pack_kernel(plan, opening, vt, *rest):
    amplitudes, rest = (rest[0], rest[1:]) if opening else (None, rest)
    outs, rest = rest[: len(plan)], rest[len(plan) :]
    if opening:
        local, rider, rows, in_sems, rider_sem = rest
    else:
        (rows,), local = rest, vt
    kw = vt.shape[0]
    vl = rows.shape[0]
    half = vl // 2
    tiles = 2 * NVIR // LANES
    chunks = in_sems.shape[0] if opening else 4
    per = vl // 2 // chunks
    z, core, plane = position()
    me = 2 * z + core

    def load(c):
        span = pl.ds(c * per * 2 * NVIR, per * 2 * NVIR)
        return pltpu.make_async_copy(vt.at[:, span], local.at[:, span], in_sems.at[c])

    if opening:
        for c in range(chunks):
            load(c).start()
        ride = pltpu.make_async_copy(amplitudes, rider, rider_sem)
        ride.start()

    def turn(pair, carry):
        base = pl.multiple_of(pair * (2 * NVIR), LANES)
        for t in range(tiles):
            block = local[:, pl.ds(pl.multiple_of(base + t * LANES, LANES), LANES)]
            turned = jnp.concatenate([block, block], axis=0).T.astype(jnp.float32)
            start = t * LANES
            if start + LANES <= NVIR:
                rows[2 * pair, start : start + LANES, :] = turned
            elif start >= NVIR:
                rows[2 * pair + 1, start - NVIR : start - NVIR + LANES, :] = turned
            else:
                cut = NVIR - start
                rows[2 * pair, start:NVIR, :] = turned[:cut]
                rows[2 * pair + 1, 0 : LANES - cut, :] = turned[cut:]
        return carry

    for c in range(chunks):
        if opening:
            load(c).wait()
        lax.fori_loop(c * per, (c + 1) * per, turn, 0, unroll=True)
    if opening:
        ride.wait()

    low = lax.broadcasted_iota(jnp.int32, (vl, LANES), 1) < kw
    for out, (kind, first, count, rides) in zip(outs, plan):
        far = far_of(kind, plane)
        base = jnp.bitwise_xor(me, far) * vl

        def gather(i, carry, out=out, base=base, first=first):
            both = []
            for h in range(2):
                a = base + 2 * (first + i) + h
                both.append(jnp.where(low, rows[:, a, :], rows[:, a + half, :]))
            spot = pl.multiple_of(i * 2 * vl, 16)
            out[pl.ds(spot, 2 * vl), :] = jnp.concatenate(both, axis=0).astype(jnp.bfloat16)
            return carry

        lax.fori_loop(0, count, gather, 0)
        if rides:
            out[count * 2 * vl :, :] = rider[...]


def pack(vt, plan, vl, amplitudes=None):
    opening = amplitudes is not None
    extra = amplitudes.shape[0] if opening else 0
    vmem = pl.BlockSpec(memory_space=pltpu.VMEM)
    hbm = pl.BlockSpec(memory_space=pltpu.HBM)
    chunks = 7
    shapes = [
        jax.ShapeDtypeStruct((count * 2 * vl + extra * rides, LANES), jnp.bfloat16) for _, _, count, rides in plan
    ]
    scratch = [pltpu.VMEM((vl, NVIR, LANES), jnp.float32)]
    if opening:
        shapes += [jax.ShapeDtypeStruct(x.shape, x.dtype) for x in (vt, amplitudes)]
        scratch += [pltpu.SemaphoreType.DMA((chunks,)), pltpu.SemaphoreType.DMA]
    return pl.pallas_call(
        functools.partial(pack_kernel, plan, opening),
        in_specs=[hbm] * 2 if opening else [vmem],
        out_specs=[vmem] * len(shapes),
        out_shape=shapes,
        scratch_shapes=scratch,
        compiler_params=pltpu.CompilerParams(vmem_limit_bytes=(48 if opening else 20) * 2**20),
        cost_estimate=pl.CostEstimate(flops=0, bytes_accessed=1024, transcendentals=0),
    )(vt, *([amplitudes] if opening else []))


def combine_kernel(sources, first, count, opening, vt, *rest):
    arrivals, rest = rest[: len(sources)], rest[len(sources) :]
    if opening:
        own, across, out, lhs, direct, turned, made, out_sems, tall = rest
    else:
        lhs, direct, _, out, turned, made, out_sems = rest
    kw = vt.shape[0]
    pairs = out.shape[0]
    n_dev = turned.shape[1] // 2
    vl = NVIR // n_dev
    steps = vl // 4
    width = 2 * NVIR
    z, core, plane = position()
    me = 2 * z + core

    if opening:
        size = own.shape[0]
        tall[plane, z] = own[...]
        tall[1 - plane, z] = across[...]
        for ref, (kind, mine, start, at, _) in zip(arrivals, sources):
            if kind in ("near", "same", "cross") and start == 0 and at == 0:
                side = plane if mine else 1 - plane
                tall[side, jnp.bitwise_xor(z, far_of(kind, side) // 2)] = ref[ref.shape[0] - size :, :]
        row = lax.broadcasted_iota(jnp.int32, (pairs, LANES), 0)
        col = lax.broadcasted_iota(jnp.int32, (pairs, LANES), 1)
        occ_i, occ_j = row // NOCC, row % NOCC
        per = pairs // NOCC
        zeros = jnp.zeros((kw, pairs), jnp.bfloat16)
        left = jnp.zeros((pairs, LANES), jnp.float32)
        right = jnp.zeros((pairs, LANES), jnp.float32)
        same = jnp.zeros((pairs, kw), jnp.float32)
        for part in range(2):
            block = tall[part].reshape(kw, pairs)
            swap = (occ_j // per == part) & (col == (occ_j % per) * NOCC + plane * per + occ_i)
            pick = jnp.where(swap, 1.0, 0.0).astype(jnp.bfloat16)
            left += lax.dot_general(pick, jnp.concatenate([block, zeros], axis=0), NT, preferred_element_type=jnp.float32)
            right += lax.dot_general(pick, jnp.concatenate([zeros, block], axis=0), NT, preferred_element_type=jnp.float32)
            keep = jnp.where((row == col) & (plane == part), 1.0, 0.0).astype(jnp.bfloat16)
            same += lax.dot_general(keep, block, NT, preferred_element_type=jnp.float32)
        lhs[:pairs, :] = left.astype(jnp.bfloat16)
        lhs[pairs:, :] = right.astype(jnp.bfloat16)
        direct[...] = same.astype(jnp.bfloat16)

    def put(h, m):
        spot = pl.ds((first + m + steps * h) * width, width)
        return pltpu.make_async_copy(made.at[h, m], out.at[:, spot], out_sems.at[h, m])

    for m in range(count):
        buffer = turned.at[m % turned.shape[0]]
        for ref, (kind, mine, start, at, size) in zip(arrivals, sources):
            if at <= m < at + size:
                q = jnp.bitwise_xor(me, far_of(kind, plane if mine else 1 - plane))
                block = ref[(start + m - at) * 2 * vl : (start + m - at + 1) * 2 * vl, :].astype(jnp.float32)
                buffer[q] = block[:vl]
                buffer[q + n_dev] = block[vl:]
        rhs = buffer[...].reshape(2 * NVIR, LANES).astype(jnp.bfloat16)
        both = lax.dot_general(lhs[...], rhs, NT, preferred_element_type=jnp.float32)
        for h in range(2):
            begin = (first + m + steps * h) * width
            ladder = lax.dot_general(direct[...], vt[:, begin : begin + width], NN, preferred_element_type=jnp.float32)
            made[h, m] = ladder + both[h * pairs : (h + 1) * pairs]
            put(h, m).start()
    for m in range(count):
        for h in range(2):
            put(h, m).wait()


def combine(vt, arrivals, sources, first, count, vl, pairs, opening=None, later=None):
    kw, width, n_dev = vt.shape[0], 2 * NVIR, NVIR // vl
    anywhere = pl.BlockSpec(memory_space=pl.ANY)
    vmem = pl.BlockSpec(memory_space=pltpu.VMEM)
    out_shape = jax.ShapeDtypeStruct((pairs, vl * NVIR), jnp.float32)
    scratch = [
        pltpu.VMEM((2, 2 * n_dev, vl, LANES), jnp.float32),
        pltpu.VMEM((2, count, pairs, width), jnp.float32),
        pltpu.SemaphoreType.DMA((2, count)),
    ]
    if opening is not None:
        extra = list(opening)
        specs = [vmem] * 2
        outs = [out_shape, jax.ShapeDtypeStruct((2 * pairs, LANES), jnp.bfloat16), jax.ShapeDtypeStruct((pairs, kw), jnp.bfloat16)]
        out_specs = [anywhere, vmem, vmem]
        scratch += [pltpu.VMEM((2, kw // opening[0].shape[0], *opening[0].shape), jnp.bfloat16)]
        aliases = {}
    else:
        extra = list(later)
        specs = [vmem, vmem, anywhere]
        outs, out_specs = out_shape, anywhere
        aliases = {1 + len(arrivals) + 2: 0}
    return pl.pallas_call(
        functools.partial(combine_kernel, sources, first, count, opening is not None),
        in_specs=[vmem] * (1 + len(arrivals)) + specs,
        out_specs=out_specs,
        out_shape=outs,
        scratch_shapes=scratch,
        input_output_aliases=aliases,
        compiler_params=pltpu.CompilerParams(vmem_limit_bytes=20 * 2**20),
        cost_estimate=pl.CostEstimate(flops=0, bytes_accessed=1024, transcendentals=0),
    )(vt, *arrivals, *extra)


def shards_fast(amplitudes, integrals):
    pairs = amplitudes.shape[0]
    vl = integrals.shape[0] // NVIR
    steps = vl // 4
    everyone = [(z, x, s) for z in range(4) for x in range(2) for s in range(2)]

    def number(z, x, s):
        return (z * 2 + x) * 2 + s

    def send(x, kind):
        def to(z, plane, s):
            if kind == "core":
                return number(z, plane, 1 - s)
            if kind == "plane":
                return number(z, 1 - plane, s)
            if kind == "near":
                return number(z ^ 1, plane, s ^ plane)
            cross = kind == "cross"
            return number(z ^ (2 + (plane ^ cross)), plane, s ^ cross)

        return lax.ppermute(x, ("blk", "occ", "sub"), [(number(*d), to(*d)) for d in everyone])

    values = {}

    def result(name):
        if name not in values:
            values[name] = make(name)
        return values[name]

    def hold(x, name):
        for first in AFTER.get(name, ()):
            values[first], x = lax.optimization_barrier((result(first), x))
        return x

    def make(name):
        if name == "head":
            plan = [(kind, first, count, first == 0) for kind, first, count, opening in MESSAGES if opening]
            return pack(integrals.T, plan, vl, amplitudes.T)
        if name == "across":
            return send(hold(result("head")[-1], name), "plane")
        if name == "tail":
            plan = [("core", 0, steps, False), ("own", 0, steps, False)]
            plan += [(kind, first, count, False) for kind, first, count, opening in MESSAGES if not opening]
            return pack(hold(result("head")[-2], name), plan, vl)
        if name == "core":
            return send(hold(result("tail")[0], name), "core")
        if name == "own":
            return result("tail")[1]
        index = int(name[1:])
        if name[0] == "x":
            return send(hold(result(f"z{index}"), name), "plane")
        kind, _, _, opening = MESSAGES[index]
        place = sum(message[3] == opening for message in MESSAGES[:index])
        return send(hold(result("head")[place] if opening else result("tail")[2 + place], name), kind)

    pieces = []
    for first, count in reversed(PIECES):
        names, sources = ["own", "core"], [("own", True, first, 0, count), ("core", True, first, 0, count)]
        for n, (kind, start, size, _) in enumerate(MESSAGES):
            low, high = max(first, start), min(first + count, start + size)
            if low < high:
                names += [f"z{n}", f"x{n}"]
                sources += [(kind, mine, low - start, low - first, high - low) for mine in (True, False)]
        pieces.append(([result(name) for name in names], sources, first, count))
    vt, own = result("head")[-2:]
    out, lhs, direct = combine(vt, *pieces.pop(), vl, pairs, opening=(own, result("across")))
    while pieces:
        out = combine(vt, *pieces.pop(), vl, pairs, later=(lhs, direct, out))
    return out


def shards_any(amplitudes, integrals):
    pairs, columns = amplitudes.shape[0], integrals.shape[1]
    vl = integrals.shape[0] // NVIR
    per = pairs // NOCC
    swapped = lax.all_to_all(
        integrals.reshape(vl, NVIR, columns), ("blk", "sub"), split_axis=1, concat_axis=0, tiled=True
    )
    swapped = jnp.transpose(swapped, (1, 0, 2)).reshape(vl * NVIR, columns)
    whole = lax.all_gather(amplitudes, "blk", axis=1, tiled=True)
    every = lax.all_gather(whole, "occ", axis=0, tiled=True).reshape(NOCC, NOCC, columns)
    mine = lax.dynamic_slice_in_dim(every, lax.axis_index("occ") * per, per, axis=1)
    mine = jnp.transpose(mine, (1, 0, 2)).reshape(pairs, columns)
    return lax.dot_general(whole, integrals, NT, preferred_element_type=jnp.float32) + lax.dot_general(
        mine, swapped, NT, preferred_element_type=jnp.float32
    )


def shards(amplitudes, integrals):
    vl = integrals.shape[0] // NVIR
    fits = NVIR == 8 * vl and integrals.shape[1] * 2 == LANES and amplitudes.shape[0] == LANES
    fits = fits and lax.axis_size("blk") == 4 and lax.axis_size("sub") == 2 and lax.axis_size("occ") == 2
    return (shards_fast if fits else shards_any)(amplitudes, integrals)


def solution(mesh):
    placed = (P(("groups", "occ"), "blk"), P(("groups", "blk", "sub"), None))
    return jax.shard_map(
        shards,
        mesh=mesh,
        in_specs=placed,
        out_specs=P(("groups", "occ"), ("blk", "sub")),
        check_vma=False,
    )
```

```python
import functools

import jax
import jax.numpy as jnp
from jax import lax
from jax.experimental import pallas as pl
from jax.experimental.pallas import tpu as pltpu
from jax.sharding import PartitionSpec as P

NOCC = 16
NVIR = 448
LANES = 128
NT = (((1,), (1,)), ((), ()))
NN = (((1,), (0,)), ((), ()))

MESSAGES = (
    ("same", 0, 6, True),
    ("cross", 0, 10, True),
    ("near", 0, 14, True),
    ("same", 6, 5, False),
    ("same", 11, 3, False),
    ("cross", 10, 4, False),
)
PIECES = ((0, 6), (6, 4), (10, 4))
AFTER = {"z3": ("z0",), "z5": ("z1",), "z4": ("x0",), "x1": ("x0",), "tail": ("across",)}


def position():
    return lax.axis_index("blk"), lax.axis_index("sub"), lax.axis_index("occ")


def far_of(kind, plane):
    if kind == "own":
        return 0
    if kind == "core":
        return 1
    if kind == "near":
        return 2 + plane
    cross = int(kind == "cross")
    return 2 * (2 + jnp.bitwise_xor(plane, cross)) + cross


def pack_kernel(plan, opening, vt, *rest):
    amplitudes, rest = (rest[0], rest[1:]) if opening else (None, rest)
    outs, rest = rest[: len(plan)], rest[len(plan) :]
    if opening:
        local, rider, rows, in_sems, rider_sem = rest
    else:
        (rows,), local = rest, vt
    kw = vt.shape[0]
    vl = rows.shape[0]
    half = vl // 2
    tiles = 2 * NVIR // LANES
    chunks = in_sems.shape[0] if opening else 4
    per = vl // 2 // chunks
    z, core, plane = position()
    me = 2 * z + core

    def load(c):
        span = pl.ds(c * per * 2 * NVIR, per * 2 * NVIR)
        return pltpu.make_async_copy(vt.at[:, span], local.at[:, span], in_sems.at[c])

    if opening:
        for c in range(chunks):
            load(c).start()
        ride = pltpu.make_async_copy(amplitudes, rider, rider_sem)
        ride.start()

    def turn(pair, carry):
        base = pl.multiple_of(pair * (2 * NVIR), LANES)
        for t in range(tiles):
            block = local[:, pl.ds(pl.multiple_of(base + t * LANES, LANES), LANES)]
            turned = jnp.concatenate([block, block], axis=0).T.astype(jnp.float32)
            start = t * LANES
            if start + LANES <= NVIR:
                rows[2 * pair, start : start + LANES, :] = turned
            elif start >= NVIR:
                rows[2 * pair + 1, start - NVIR : start - NVIR + LANES, :] = turned
            else:
                cut = NVIR - start
                rows[2 * pair, start:NVIR, :] = turned[:cut]
                rows[2 * pair + 1, 0 : LANES - cut, :] = turned[cut:]
        return carry

    for c in range(chunks):
        if opening:
            load(c).wait()
        lax.fori_loop(c * per, (c + 1) * per, turn, 0, unroll=True)
    if opening:
        ride.wait()

    low = lax.broadcasted_iota(jnp.int32, (vl, LANES), 1) < kw
    for out, (kind, first, count, rides) in zip(outs, plan):
        far = far_of(kind, plane)
        base = jnp.bitwise_xor(me, far) * vl

        def gather(i, carry, out=out, base=base, first=first):
            both = []
            for h in range(2):
                a = base + 2 * (first + i) + h
                both.append(jnp.where(low, rows[:, a, :], rows[:, a + half, :]))
            spot = pl.multiple_of(i * 2 * vl, 16)
            out[pl.ds(spot, 2 * vl), :] = jnp.concatenate(both, axis=0).astype(jnp.bfloat16)
            return carry

        lax.fori_loop(0, count, gather, 0, unroll=2)
        if rides:
            out[count * 2 * vl :, :] = rider[...]


def pack(vt, plan, vl, amplitudes=None):
    opening = amplitudes is not None
    extra = amplitudes.shape[0] if opening else 0
    vmem = pl.BlockSpec(memory_space=pltpu.VMEM)
    hbm = pl.BlockSpec(memory_space=pltpu.HBM)
    chunks = 4
    shapes = [
        jax.ShapeDtypeStruct((count * 2 * vl + extra * rides, LANES), jnp.bfloat16) for _, _, count, rides in plan
    ]
    scratch = [pltpu.VMEM((vl, NVIR, LANES), jnp.float32)]
    if opening:
        shapes += [jax.ShapeDtypeStruct(x.shape, x.dtype) for x in (vt, amplitudes)]
        scratch += [pltpu.SemaphoreType.DMA((chunks,)), pltpu.SemaphoreType.DMA]
    return pl.pallas_call(
        functools.partial(pack_kernel, plan, opening),
        in_specs=[hbm] * 2 if opening else [vmem],
        out_specs=[vmem] * len(shapes),
        out_shape=shapes,
        scratch_shapes=scratch,
        compiler_params=pltpu.CompilerParams(vmem_limit_bytes=(48 if opening else 20) * 2**20),
        cost_estimate=pl.CostEstimate(flops=0, bytes_accessed=1024, transcendentals=0),
    )(vt, *([amplitudes] if opening else []))


def combine_kernel(sources, first, count, opening, vt, *rest):
    arrivals, rest = rest[: len(sources)], rest[len(sources) :]
    if opening:
        own, across, out, lhs, direct, turned, made, out_sems, tall = rest
    else:
        lhs, direct, _, out, turned, made, out_sems = rest
    kw = vt.shape[0]
    pairs = out.shape[0]
    n_dev = turned.shape[1] // 2
    vl = NVIR // n_dev
    steps = vl // 4
    width = 2 * NVIR
    z, core, plane = position()
    me = 2 * z + core

    if opening:
        size = own.shape[0]
        tall[plane, z] = own[...]
        tall[1 - plane, z] = across[...]
        for ref, (kind, mine, start, at, _) in zip(arrivals, sources):
            if kind in ("near", "same", "cross") and start == 0 and at == 0:
                side = plane if mine else 1 - plane
                tall[side, jnp.bitwise_xor(z, far_of(kind, side) // 2)] = ref[ref.shape[0] - size :, :]
        row = lax.broadcasted_iota(jnp.int32, (pairs, LANES), 0)
        col = lax.broadcasted_iota(jnp.int32, (pairs, LANES), 1)
        occ_i, occ_j = row // NOCC, row % NOCC
        per = pairs // NOCC
        zeros = jnp.zeros((kw, pairs), jnp.bfloat16)
        left = jnp.zeros((pairs, LANES), jnp.float32)
        right = jnp.zeros((pairs, LANES), jnp.float32)
        same = jnp.zeros((pairs, kw), jnp.float32)
        for part in range(2):
            block = tall[part].reshape(kw, pairs)
            swap = (occ_j // per == part) & (col == (occ_j % per) * NOCC + plane * per + occ_i)
            pick = jnp.where(swap, 1.0, 0.0).astype(jnp.bfloat16)
            left += lax.dot_general(pick, jnp.concatenate([block, zeros], axis=0), NT, preferred_element_type=jnp.float32)
            right += lax.dot_general(pick, jnp.concatenate([zeros, block], axis=0), NT, preferred_element_type=jnp.float32)
            keep = jnp.where((row == col) & (plane == part), 1.0, 0.0).astype(jnp.bfloat16)
            same += lax.dot_general(keep, block, NT, preferred_element_type=jnp.float32)
        lhs[:pairs, :] = left.astype(jnp.bfloat16)
        lhs[pairs:, :] = right.astype(jnp.bfloat16)
        direct[...] = same.astype(jnp.bfloat16)

    def put(h, m):
        spot = pl.ds((first + m + steps * h) * width, width)
        return pltpu.make_async_copy(made.at[h, m], out.at[:, spot], out_sems.at[h, m])

    for m in range(count):
        buffer = turned.at[m % turned.shape[0]]
        for ref, (kind, mine, start, at, size) in zip(arrivals, sources):
            if at <= m < at + size:
                q = jnp.bitwise_xor(me, far_of(kind, plane if mine else 1 - plane))
                block = ref[(start + m - at) * 2 * vl : (start + m - at + 1) * 2 * vl, :].astype(jnp.float32)
                buffer[q] = block[:vl]
                buffer[q + n_dev] = block[vl:]
        rhs = buffer[...].reshape(2 * NVIR, LANES).astype(jnp.bfloat16)
        both = lax.dot_general(lhs[...], rhs, NT, preferred_element_type=jnp.float32)
        for h in range(2):
            begin = (first + m + steps * h) * width
            ladder = lax.dot_general(direct[...], vt[:, begin : begin + width], NN, preferred_element_type=jnp.float32)
            made[h, m] = ladder + both[h * pairs : (h + 1) * pairs]
            put(h, m).start()
    for m in range(count):
        for h in range(2):
            put(h, m).wait()


def combine(vt, arrivals, sources, first, count, vl, pairs, opening=None, later=None):
    kw, width, n_dev = vt.shape[0], 2 * NVIR, NVIR // vl
    anywhere = pl.BlockSpec(memory_space=pl.ANY)
    vmem = pl.BlockSpec(memory_space=pltpu.VMEM)
    out_shape = jax.ShapeDtypeStruct((pairs, vl * NVIR), jnp.float32)
    scratch = [
        pltpu.VMEM((2, 2 * n_dev, vl, LANES), jnp.float32),
        pltpu.VMEM((2, count, pairs, width), jnp.float32),
        pltpu.SemaphoreType.DMA((2, count)),
    ]
    if opening is not None:
        extra = list(opening)
        specs = [vmem] * 2
        outs = [out_shape, jax.ShapeDtypeStruct((2 * pairs, LANES), jnp.bfloat16), jax.ShapeDtypeStruct((pairs, kw), jnp.bfloat16)]
        out_specs = [anywhere, vmem, vmem]
        scratch += [pltpu.VMEM((2, kw // opening[0].shape[0], *opening[0].shape), jnp.bfloat16)]
        aliases = {}
    else:
        extra = list(later)
        specs = [vmem, vmem, anywhere]
        outs, out_specs = out_shape, anywhere
        aliases = {1 + len(arrivals) + 2: 0}
    return pl.pallas_call(
        functools.partial(combine_kernel, sources, first, count, opening is not None),
        in_specs=[vmem] * (1 + len(arrivals)) + specs,
        out_specs=out_specs,
        out_shape=outs,
        scratch_shapes=scratch,
        input_output_aliases=aliases,
        compiler_params=pltpu.CompilerParams(vmem_limit_bytes=20 * 2**20),
        cost_estimate=pl.CostEstimate(flops=0, bytes_accessed=1024, transcendentals=0),
    )(vt, *arrivals, *extra)


def shards_fast(amplitudes, integrals):
    pairs = amplitudes.shape[0]
    vl = integrals.shape[0] // NVIR
    steps = vl // 4
    everyone = [(z, x, s) for z in range(4) for x in range(2) for s in range(2)]

    def number(z, x, s):
        return (z * 2 + x) * 2 + s

    def send(x, kind):
        def to(z, plane, s):
            if kind == "core":
                return number(z, plane, 1 - s)
            if kind == "plane":
                return number(z, 1 - plane, s)
            if kind == "near":
                return number(z ^ 1, plane, s ^ plane)
            cross = kind == "cross"
            return number(z ^ (2 + (plane ^ cross)), plane, s ^ cross)

        return lax.ppermute(x, ("blk", "occ", "sub"), [(number(*d), to(*d)) for d in everyone])

    values = {}

    def result(name):
        if name not in values:
            values[name] = make(name)
        return values[name]

    def hold(x, name):
        for first in AFTER.get(name, ()):
            values[first], x = lax.optimization_barrier((result(first), x))
        return x

    def make(name):
        if name == "head":
            plan = [(kind, first, count, first == 0) for kind, first, count, opening in MESSAGES if opening]
            return pack(integrals.T, plan, vl, amplitudes.T)
        if name == "across":
            return send(hold(result("head")[-1], name), "plane")
        if name == "tail":
            plan = [("core", 0, steps, False), ("own", 0, steps, False)]
            plan += [(kind, first, count, False) for kind, first, count, opening in MESSAGES if not opening]
            return pack(hold(result("head")[-2], name), plan, vl)
        if name == "core":
            return send(hold(result("tail")[0], name), "core")
        if name == "own":
            return result("tail")[1]
        index = int(name[1:])
        if name[0] == "x":
            return send(hold(result(f"z{index}"), name), "plane")
        kind, _, _, opening = MESSAGES[index]
        place = sum(message[3] == opening for message in MESSAGES[:index])
        return send(hold(result("head")[place] if opening else result("tail")[2 + place], name), kind)

    pieces = []
    for first, count in reversed(PIECES):
        names, sources = ["own", "core"], [("own", True, first, 0, count), ("core", True, first, 0, count)]
        for n, (kind, start, size, _) in enumerate(MESSAGES):
            low, high = max(first, start), min(first + count, start + size)
            if low < high:
                names += [f"z{n}", f"x{n}"]
                sources += [(kind, mine, low - start, low - first, high - low) for mine in (True, False)]
        pieces.append(([result(name) for name in names], sources, first, count))
    vt, own = result("head")[-2:]
    out, lhs, direct = combine(vt, *pieces.pop(), vl, pairs, opening=(own, result("across")))
    while pieces:
        out = combine(vt, *pieces.pop(), vl, pairs, later=(lhs, direct, out))
    return out


def shards_any(amplitudes, integrals):
    pairs, columns = amplitudes.shape[0], integrals.shape[1]
    vl = integrals.shape[0] // NVIR
    per = pairs // NOCC
    swapped = lax.all_to_all(
        integrals.reshape(vl, NVIR, columns), ("blk", "sub"), split_axis=1, concat_axis=0, tiled=True
    )
    swapped = jnp.transpose(swapped, (1, 0, 2)).reshape(vl * NVIR, columns)
    whole = lax.all_gather(amplitudes, "blk", axis=1, tiled=True)
    every = lax.all_gather(whole, "occ", axis=0, tiled=True).reshape(NOCC, NOCC, columns)
    mine = lax.dynamic_slice_in_dim(every, lax.axis_index("occ") * per, per, axis=1)
    mine = jnp.transpose(mine, (1, 0, 2)).reshape(pairs, columns)
    return lax.dot_general(whole, integrals, NT, preferred_element_type=jnp.float32) + lax.dot_general(
        mine, swapped, NT, preferred_element_type=jnp.float32
    )


def shards(amplitudes, integrals):
    vl = integrals.shape[0] // NVIR
    fits = NVIR == 8 * vl and integrals.shape[1] * 2 == LANES and amplitudes.shape[0] == LANES
    fits = fits and lax.axis_size("blk") == 4 and lax.axis_size("sub") == 2 and lax.axis_size("occ") == 2
    return (shards_fast if fits else shards_any)(amplitudes, integrals)


def solution(mesh):
    placed = (P(("groups", "occ"), "blk"), P(("groups", "blk", "sub"), None))
    return jax.shard_map(
        shards,
        mesh=mesh,
        in_specs=placed,
        out_specs=P(("groups", "occ"), ("blk", "sub")),
        check_vma=False,
    )
```
